512 devices in a mesh: seq: 64 (over x, y, core), section: 8 (over z).
Axes of the slice: x: 4, y: 8, z: 8, core: 2. Of those that a mesh axis runs over, the one named last changes fastest.
Arguments:
- encoded: bfloat16 [8, 4096, 1408], P(None, 'seq'), may hold values from -6 to 6
- conv_weight: bfloat16 [8, 4224, 1408], P('section', 'seq'), may hold values from -0.09375 to 0.09375
- section_gain: float32 [8, 1408], P('section'), may hold values from 0.4 to 1.6
- head_gain: float32 [1408], replicated, may hold values from 0.4 to 1.6
- head_weight: bfloat16 [1408, 1408], P('seq'), may hold values from -0.15625 to 0.15625
- pair_donor: int32 [8, 64, 64], P('section', 'seq'), may hold values from 0 to 63
- pair_acceptor: int32 [8, 64, 64], P('section', 'seq'), may hold values from 0 to 63
- pair_count: int32 [8, 64, 4], P('section', 'seq'), may hold values from 0 to 16, as said below
- pair_cotangent: float32 [8, 64, 64], P('section', 'seq'), may hold values from -48 to 48
Outputs:
- stash: bfloat16 [8, 8, 4096, 1408], P('section', None, 'seq')
- junction_grad: float32 [8, 4096, 1408], P('section', 'seq')
The draws below stay inside these ranges and needn't reach their ends.
Inputs may be any that keep to these rules, and one draw needn't show every extreme that they name: pair_count[m, i, o] is 0 where i + o >= 64; in every micro-batch some slab holds exactly 16 live slots for some reach o >= 1.
All inputs are finite; a program needn't handle non-finite values.
Results may differ from the reference program's by a relative error of at most 0.013.
Values may be sent and summed in bfloat16 or wider, within the bound.
No kernel may reach another device: no remote copies, remote signals or barrier semaphores. Data moves between devices by JAX's collectives and lax.ppermute only.
A program may use at most 128 MiB of HBM per device.

```python
import jax
import jax.numpy as jnp
from jax import lax

CHANNEL_COUNT = 1408
SLAB = 64
REACH = 4
CAP = 16
DILATION_STEP = 32
SLABS = 64
POSITION_COUNT = 4096
MICRO = 8
N_SECTION = 8


def draw_pair_count(key, part):
    key = jax.random.fold_in(key, 7)
    key_dense, key_base, key_slab, key_reach = jax.random.split(key, 4)
    density = jax.random.randint(key_dense, (MICRO, SLABS, 1), 1, 5)
    base = jax.random.randint(key_base, (MICRO, SLABS, REACH), CAP // 8, CAP // 4 + 1)
    counts = jnp.minimum(density * base, CAP)
    slab_ids = jnp.arange(SLABS)[None, :, None]
    reach_ids = jnp.arange(REACH)[None, None, :]
    counts = jnp.where(slab_ids + reach_ids < SLABS, counts, 0)
    full_slab = jax.random.randint(key_slab, (MICRO, 1, 1), 0, SLABS - REACH + 1)
    full_reach = jax.random.randint(key_reach, (MICRO, 1, 1), 1, REACH)
    counts = jnp.where((slab_ids == full_slab) & (reach_ids == full_reach), CAP, counts)
    return counts.astype(jnp.int32)


def with_ends(values, stream_key, smallest, high):
    spot = [jax.random.randint(jax.random.fold_in(stream_key, axis), (), 0, length) for axis, length in enumerate(values.shape)]
    longest = values.shape.index(max(values.shape))
    next_to = spot[:longest] + [(spot[longest] + 1) % values.shape[longest]] + spot[longest + 1:]
    return values.at[tuple(spot)].set(smallest).at[tuple(next_to)].set(high)


def block_levels(rng, shape, shards, low, high):
    def one(dim, parts):
        steps = jax.random.uniform(jax.random.fold_in(jax.random.fold_in(rng, 6), dim), (parts,), jnp.float32, low / len(shards), high / len(shards))
        return jnp.repeat(jnp.exp(steps), shape[dim] // parts).reshape((-1,) + (1,) * (len(shape) - dim - 1))

    level = one(*shards[0])
    for cut in shards[1:]:
        level = level * one(*cut)
    return level


def gaussian(stream_key, dims, scale, reach, shards=(), held_as=jnp.bfloat16):
    factor_of = block_levels(stream_key, dims, shards, -0.22, 0.18) if shards else 1.0
    entries = jax.random.normal(stream_key, dims, jnp.float32) * scale * factor_of
    return jnp.minimum(jnp.maximum(entries, -reach), reach).astype(held_as)


def setup_inputs(seed: int = 0) -> dict:
    arg_keys = jax.random.split(jax.random.key(seed), 10)
    encoded = gaussian(arg_keys[0], (MICRO, POSITION_COUNT, CHANNEL_COUNT), 1.0, 6.0, ((1, 64),))
    conv_weight = gaussian(arg_keys[1], (N_SECTION, 3 * CHANNEL_COUNT, CHANNEL_COUNT), (3 * CHANNEL_COUNT) ** -0.5, 0.09375, ((0, 8), (1, 64)))
    section_gain = jnp.clip(1.0 + 0.12 * jax.random.normal(arg_keys[2], (N_SECTION, CHANNEL_COUNT), jnp.float32), 0.4, 1.6)
    head_gain = jnp.clip(1.0 + 0.12 * jax.random.normal(arg_keys[3], (CHANNEL_COUNT,), jnp.float32), 0.4, 1.6)
    head_weight = gaussian(arg_keys[4], (CHANNEL_COUNT, CHANNEL_COUNT), CHANNEL_COUNT ** -0.5, 0.15625, ((0, 64),))
    pair_donor = with_ends(jax.random.randint(arg_keys[5], (MICRO, SLABS, REACH * CAP), 0, SLAB), jax.random.fold_in(arg_keys[5], 1), 0, SLAB - 1).astype(jnp.int32)
    pair_acceptor = with_ends(jax.random.randint(arg_keys[6], (MICRO, SLABS, REACH * CAP), 0, SLAB), jax.random.fold_in(arg_keys[6], 1), 0, SLAB - 1).astype(jnp.int32)
    pair_count = draw_pair_count(jax.random.fold_in(arg_keys[9], 71), 0)
    pair_cotangent = gaussian(arg_keys[8], (MICRO, SLABS, REACH * CAP), 8.0, 48.0, ((0, 8), (1, 64)), jnp.float32)
    return {"encoded": encoded, "conv_weight": conv_weight, "section_gain": section_gain, "head_gain": head_gain, "head_weight": head_weight, "pair_donor": pair_donor, "pair_acceptor": pair_acceptor, "pair_count": pair_count, "pair_cotangent": pair_cotangent}


def rms_scaled(values, gains):
    return values * lax.rsqrt(lax.optimization_barrier(jnp.mean(values * values, axis=-1, keepdims=True)) + 1e-06) * gains.astype(jnp.float32)

def conv_block(acts, weight, gains):
    normed = rms_scaled(acts.astype(jnp.float32), gains).astype(jnp.bfloat16)
    border_width = jnp.zeros((DILATION_STEP, CHANNEL_COUNT), jnp.bfloat16)
    padded_input = jnp.concatenate([border_width, normed, border_width], axis=0)
    kernel_tap_rows = jnp.concatenate([padded_input[:POSITION_COUNT], padded_input[DILATION_STEP:DILATION_STEP + POSITION_COUNT], padded_input[2 * DILATION_STEP:2 * DILATION_STEP + POSITION_COUNT]], axis=1)
    mixed = jnp.dot(kernel_tap_rows, weight, preferred_element_type=jnp.float32)
    return (acts.astype(jnp.float32) + jax.nn.gelu(mixed)).astype(jnp.bfloat16)

def reference(encoded, conv_weight, section_gain, head_gain, head_weight, pair_donor, pair_acceptor, pair_count, pair_cotangent):

    def through(acts):
        kept = []
        for section_pos in range(N_SECTION):
            acts = conv_block(acts, conv_weight[section_pos], section_gain[section_pos])
            kept.append(acts)
        return jnp.stack(kept)
    stashed = jnp.transpose(lax.map(through, encoded), (1, 0, 2, 3))
    scale = CHANNEL_COUNT ** (-0.5)
    slot = jnp.arange(REACH * CAP, dtype=jnp.int32)
    reach_of = slot // CAP
    lane = slot % CAP
    slab_ids = jnp.arange(SLABS, dtype=jnp.int32)[:, None]

    def junctions(items):
        final, skipped, donors, acceptors, counts, cotangents = items
        embed = rms_scaled(final.astype(jnp.float32) + skipped.astype(jnp.float32), head_gain).astype(jnp.bfloat16)
        queries = jnp.dot(embed, head_weight, preferred_element_type=jnp.float32).astype(jnp.bfloat16)
        valid = lane[None, :] < counts[:, reach_of]
        weighted = jnp.where(valid, cotangents, jnp.zeros_like(cotangents)).reshape(-1, 1)
        donor_pos = (slab_ids * SLAB + donors).reshape(-1).astype(jnp.int32)
        target_slab = jnp.minimum(slab_ids + reach_of[None, :], SLABS - 1)
        accept_pos = (target_slab * SLAB + acceptors[target_slab, slot[None, :]]).reshape(-1).astype(jnp.int32)
        sent = (weighted * queries[donor_pos].astype(jnp.float32) * scale).astype(jnp.bfloat16)
        from_acc = jnp.zeros((POSITION_COUNT, CHANNEL_COUNT), jnp.float32).at[accept_pos].add(sent.astype(jnp.float32))
        query_grad = jnp.zeros((POSITION_COUNT, CHANNEL_COUNT), jnp.float32).at[donor_pos].add(weighted * embed[accept_pos].astype(jnp.float32) * scale)
        return jnp.dot(query_grad.astype(jnp.bfloat16), head_weight.T, preferred_element_type=jnp.float32) + from_acc
    junction_grad = lax.map(junctions, (stashed[N_SECTION - 1], stashed[0], pair_donor, pair_acceptor, pair_count, pair_cotangent))
    return (stashed, junction_grad)
```

```python
import functools

import jax
import jax.numpy as jnp
from jax import lax
from jax.experimental import pallas as pl
from jax.experimental.pallas import tpu as pltpu
from jax.sharding import PartitionSpec as P


def from_behind(shard, axis, by):
    size = lax.axis_size(axis)
    pairs = [(i, i + by) for i in range(size) if 0 <= i + by < size]
    return lax.ppermute(shard, axis, pairs)


def rms_scaled(values, gains):
    return values * lax.rsqrt(jnp.mean(values * values, axis=-1, keepdims=True) + 1e-06) * gains


def core_swap(shard):
    return lax.ppermute(shard, "seq", [(i, i ^ 1) for i in range(lax.axis_size("seq"))])


def in_core_order(first_core, mine, other, axis):
    return jnp.where(
        first_core,
        jnp.concatenate([mine, other], axis=axis),
        jnp.concatenate([other, mine], axis=axis),
    )


def gathered_columns(shard, fetched):
    count = lax.axis_size("seq")
    columns = shard.shape[1]
    first_core = lax.axis_index("seq") % 2 == 0
    left, right = shard[:, :fetched], shard[:, columns - fetched :]
    arrived = core_swap(jnp.where(first_core, right, left))
    rows = in_core_order(first_core, jnp.where(first_core, left, right), arrived, 0)
    same_core = [list(range(core, count, 2)) for core in range(2)]
    return lax.all_gather(rows, "seq", axis_index_groups=same_core, axis=0, tiled=True)


def place_kernel(core_ref, mine_ref, other_ref, weights_ref, sems):
    fetched = mine_ref.shape[1]
    shared = 2 * fetched - weights_ref.shape[1]

    def place(left_ref, right_ref):
        copies = [
            pltpu.make_async_copy(left_ref, weights_ref.at[:, :fetched], sems.at[0]),
            pltpu.make_async_copy(right_ref.at[:, shared:], weights_ref.at[:, fetched:], sems.at[1]),
        ]
        for copy in copies:
            copy.start()
        for copy in copies:
            copy.wait()

    @pl.when(core_ref[0] == 0)
    def _():
        place(mine_ref, other_ref)

    @pl.when(core_ref[0] != 0)
    def _():
        place(other_ref, mine_ref)


def placed_weights(core, mine, other, columns):
    rows = mine.shape[0]
    return pl.pallas_call(
        place_kernel,
        out_shape=pltpu.VMEM((rows, columns), mine.dtype),
        in_specs=[
            pl.BlockSpec(memory_space=pltpu.SMEM),
            pl.BlockSpec(memory_space=pl.ANY),
            pl.BlockSpec(memory_space=pl.ANY),
        ],
        out_specs=pl.BlockSpec(memory_space=pltpu.VMEM),
        scratch_shapes=[pltpu.SemaphoreType.DMA((2,))],
        compiler_params=pltpu.CompilerParams(vmem_limit_bytes=16 << 20),
        cost_estimate=pl.CostEstimate(flops=0, bytes_accessed=2 * rows * columns * 2, transcendentals=0),
    )(core, mine, other)


def block_kernel(
    wide_columns, flags_ref, weights_ref, gain_ref, incoming_ref, fresh_ref, result_ref, own_ref, taps_ref, acts_ref
):
    rows, channels = incoming_ref.shape
    kept_rows = own_ref.shape[0]
    padded_rows = taps_ref.shape[0]
    fresh, low_half, forward = (flags_ref[i] != 0 for i in range(3))
    acts = jnp.where(fresh, fresh_ref[...].astype(jnp.float32), incoming_ref[...].astype(jnp.float32))
    acts_ref[...] = acts
    normed = rms_scaled(acts, gain_ref[...])
    normed = jnp.concatenate([normed, jnp.zeros((padded_rows - rows, channels), jnp.float32)], axis=0)
    taps_ref[:, :channels] = pltpu.roll(normed, 1, 0).astype(jnp.bfloat16)
    taps_ref[:, channels : 2 * channels] = normed.astype(jnp.bfloat16)
    taps_ref[:, 2 * channels :] = pltpu.roll(normed, padded_rows - 1, 0).astype(jnp.bfloat16)

    def columns(at):
        mixed = jnp.dot(taps_ref[...], weights_ref[:, at], preferred_element_type=jnp.float32)
        result = acts_ref[:, at] + jax.nn.gelu(mixed[:rows])
        own = jnp.where(low_half, result[:kept_rows], result[rows - kept_rows :])
        own_ref[:, at] = own.astype(jnp.bfloat16)
        sent = jnp.where(forward, incoming_ref[:, at].astype(jnp.float32), result)
        result_ref[:, at] = sent.astype(jnp.bfloat16)

    whole = channels // wide_columns

    def step(i, _):
        columns(pl.ds(pl.multiple_of(i * wide_columns, wide_columns), wide_columns))
        return 0

    lax.fori_loop(0, whole, step, 0)
    if channels > whole * wide_columns:
        columns(pl.ds(whole * wide_columns, channels - whole * wide_columns))


def block(flags, weights, gains, incoming, fresh, kept_rows):
    rows, channels = incoming.shape
    padded_rows = -(-rows // 16) * 16
    vmem = pl.BlockSpec(memory_space=pltpu.VMEM)
    return pl.pallas_call(
        functools.partial(block_kernel, 256),
        out_shape=(
            jax.ShapeDtypeStruct((rows, channels), jnp.bfloat16),
            jax.ShapeDtypeStruct((kept_rows, channels), jnp.bfloat16),
        ),
        in_specs=[pl.BlockSpec(memory_space=pltpu.SMEM)] + [vmem] * 4,
        out_specs=(vmem, vmem),
        scratch_shapes=[
            pltpu.VMEM((padded_rows, weights.shape[0]), jnp.bfloat16),
            pltpu.VMEM((rows, channels), jnp.float32),
        ],
        compiler_params=pltpu.CompilerParams(vmem_limit_bytes=20 << 20),
        cost_estimate=pl.CostEstimate(
            flops=2 * rows * weights.shape[0] * channels,
            bytes_accessed=4 * rows * channels * 2,
            transcendentals=rows * channels,
        ),
    )(flags, pltpu.with_memory_space_constraint(weights, pltpu.VMEM), gains, incoming, fresh)


def on_device(
    encoded,
    conv_weight,
    section_gain,
    head_gain,
    head_weight,
    pair_donor,
    pair_acceptor,
    pair_count,
    pair_cotangent,
):
    micro_count, slab_rows, channels = encoded.shape
    sections = lax.axis_size("section")
    last = sections - 1
    section_pos = lax.axis_index("section")
    slabs = lax.axis_size("seq")
    dilation = slab_rows // 2
    half = slabs // 2
    spare = sections
    low_half = lax.axis_index("seq") < half
    halves = [list(range(half)), list(range(half, slabs))]

    fetched = -(-channels // 256) * 128
    weight_part = gathered_columns(conv_weight[0], fetched)
    def to_chains(rows):
        blocks = rows.reshape(2, dilation, channels)
        chains = lax.all_to_all(blocks, "seq", 1, 0, axis_index_groups=halves)
        return chains.reshape(slab_rows, channels)

    def to_slabs(chains):
        lead = chains.shape[:-2]
        blocks = chains.reshape(*lead, half, 2, channels)
        at = len(lead)
        rows = lax.all_to_all(blocks, "seq", at, at + 1, axis_index_groups=halves)
        return rows.reshape(*lead, slab_rows, channels)

    def own_rows(wide):
        return jnp.where(low_half, wide[..., :slab_rows, :], wide[..., spare:, :])

    mine = lax.dynamic_index_in_dim(encoded, section_pos, 0, keepdims=False)
    chains = to_chains(mine)
    edge = lax.ppermute(
        jnp.where(low_half, chains[slab_rows - spare :], chains[:spare]),
        "seq",
        [(i, (i + half) % slabs) for i in range(slabs)],
    )
    wide = jnp.where(
        low_half,
        jnp.concatenate([chains, edge], axis=0),
        jnp.concatenate([edge, chains], axis=0),
    )
    order = list(range(last - 1, -1, -1)) + [last]
    fresh = [wide if m == 0 else lax.ppermute(wide, "section", [(m, 0)]) for m in order]
    weight_part, *fresh = lax.optimization_barrier((weight_part, *fresh))
    core = (lax.axis_index("seq") % 2).astype(jnp.int32)
    weights = placed_weights(core[None], weight_part, core_swap(weight_part), channels)
    head_weight, weight_part = lax.optimization_barrier((head_weight, weight_part))
    head_parts = lax.all_gather(head_weight, "seq")

    ticks = micro_count + last
    def gathered_outputs(owns, first, count):
        held = jnp.stack(owns[first : first + count + last])
        return lax.dynamic_slice_in_dim(held, section_pos, count, 0)

    early = micro_count // 2
    results, owns, landing = [], [], []
    skip_input = 0.0
    incoming = jnp.zeros_like(wide)
    for tick in range(ticks):
        rank = tick - section_pos
        flags = jnp.stack(
            [
                (section_pos == 0) & (tick < micro_count),
                low_half,
                rank >= micro_count,
            ]
        ).astype(jnp.int32)
        result, own = block(
            flags, weights, section_gain, incoming, fresh[tick] if tick < micro_count else incoming, slab_rows
        )
        results.append(result)
        owns.append(own)
        if tick == ticks - 1:
            final = jnp.where(section_pos == last, result, incoming)
            break
        if tick >= micro_count - 1:
            home = tick - micro_count + 1 or last
            skip, result = lax.optimization_barrier((results[order.index(home)], result))
            landing.append(lax.ppermute(skip, "section", [(0, home)]))
        incoming = lax.ppermute(
            result, "section", [(i, (i + 1) % sections) for i in range(sections)]
        )
        if len(landing) > 1:
            landed, incoming = lax.optimization_barrier((landing.pop(0), incoming))
            skip_input = skip_input + landed.astype(jnp.float32)
        if tick == early - 1 + last:
            early_rows = to_slabs(gathered_outputs(owns, 0, early))
        if tick == early + 1 + last:
            head_parts, early_rows, incoming = lax.optimization_barrier((head_parts, early_rows, incoming))
            head_full = head_parts.reshape(channels, channels)
        if tick == ticks - 2:
            late_rows = to_slabs(gathered_outputs(owns, early, last - early))
    for landed in landing:
        skip_input = skip_input + landed.astype(jnp.float32)
    skip_input = skip_input + jnp.where(section_pos == 0, results[order.index(0)], 0).astype(jnp.float32)
    head_input = final.astype(jnp.float32) + skip_input
    embed = own_rows(rms_scaled(head_input, head_gain).astype(jnp.bfloat16))
    newest = functools.reduce(
        lambda total, s: jnp.where(section_pos == s, owns[last + s], total), range(1, sections), owns[last]
    )
    embed, late_rows = lax.optimization_barrier((embed, late_rows))
    embed, newest_rows = to_slabs(jnp.stack([embed, newest]))
    entered = jnp.concatenate([early_rows, late_rows, newest_rows[None]], axis=0)
    stashed = jnp.stack([entered[order.index(m)] for m in range(micro_count)])

    scale = channels ** (-0.5)
    reach_count = pair_count.shape[2]
    capacity = pair_donor.shape[2] // reach_count
    donors = pair_donor[0, 0]
    acceptors = pair_acceptor[0, 0]
    counts = pair_count[0, 0]
    cotangents = pair_cotangent[0, 0]
    answers = jnp.take(embed, acceptors, axis=0)
    returned = [answers[:capacity]]
    for reach_idx in range(1, reach_count):
        lower = reach_idx * capacity
        returned.append(from_behind(answers[lower : lower + capacity], "seq", -reach_idx))
    queries = jnp.dot(embed, head_full, preferred_element_type=jnp.float32).astype(jnp.bfloat16)
    slot = jnp.arange(reach_count * capacity, dtype=jnp.int32)
    valid = slot % capacity < jnp.repeat(counts, capacity)
    weighted = jnp.where(valid, cotangents, jnp.zeros_like(cotangents))[:, None]
    sent = (weighted * jnp.take(queries, donors, axis=0).astype(jnp.float32) * scale).astype(
        jnp.bfloat16
    )
    received = [sent[:capacity]]
    for reach_idx in range(1, reach_count):
        lower = reach_idx * capacity
        received.append(from_behind(sent[lower : lower + capacity], "seq", reach_idx))
    received = jnp.concatenate(received, axis=0)
    returned = jnp.concatenate(returned, axis=0)
    position_index = jnp.arange(slab_rows, dtype=jnp.int32)
    accept_hot = (position_index[:, None] == acceptors[None, :]).astype(jnp.bfloat16)
    from_acc = jnp.dot(accept_hot, received, preferred_element_type=jnp.float32)
    donor_onehot = (position_index[:, None] == donors[None, :]).astype(jnp.float32)
    query_grad = jnp.dot(
        donor_onehot,
        weighted * returned.astype(jnp.float32) * scale,
        precision=lax.Precision.HIGHEST,
    )
    grad_rows = (
        lax.dot_general(
            query_grad.astype(jnp.bfloat16),
            head_full,
            (((1,), (1,)), ((), ())),
            preferred_element_type=jnp.float32,
        )
        + from_acc
    )
    return (stashed[None], grad_rows[None])


def solution(mesh):
    placed = (
        P(None, "seq", None),
        P("section", "seq", None),
        P("section", None),
        P(),
        P("seq", None),
        P("section", "seq", None),
        P("section", "seq", None),
        P("section", "seq", None),
        P("section", "seq", None),
    )
    return jax.shard_map(
        on_device,
        mesh=mesh,
        in_specs=placed,
        out_specs=(P("section", None, "seq", None), P("section", "seq", None)),
        check_vma=False,
    )
```

```python
import functools

import jax
import jax.numpy as jnp
from jax import lax
from jax.experimental import pallas as pl
from jax.experimental.pallas import tpu as pltpu
from jax.sharding import PartitionSpec as P


def from_behind(shard, axis, by):
    size = lax.axis_size(axis)
    pairs = [(i, i + by) for i in range(size) if 0 <= i + by < size]
    return lax.ppermute(shard, axis, pairs)


def rms_scaled(values, gains):
    return values * lax.rsqrt(jnp.mean(values * values, axis=-1, keepdims=True) + 1e-06) * gains


def core_swap(shard):
    return lax.ppermute(shard, "seq", [(i, i ^ 1) for i in range(lax.axis_size("seq"))])


def in_core_order(first_core, mine, other, axis):
    return jnp.where(
        first_core,
        jnp.concatenate([mine, other], axis=axis),
        jnp.concatenate([other, mine], axis=axis),
    )


def gathered_columns(shard, fetched):
    count = lax.axis_size("seq")
    columns = shard.shape[1]
    first_core = lax.axis_index("seq") % 2 == 0
    left, right = shard[:, :fetched], shard[:, columns - fetched :]
    arrived = core_swap(jnp.where(first_core, right, left))
    rows = in_core_order(first_core, jnp.where(first_core, left, right), arrived, 0)
    same_core = [list(range(core, count, 2)) for core in range(2)]
    return lax.all_gather(rows, "seq", axis_index_groups=same_core, axis=0, tiled=True)


def place_kernel(core_ref, mine_ref, other_ref, weights_ref, sems):
    fetched = mine_ref.shape[1]
    shared = 2 * fetched - weights_ref.shape[1]

    def place(left_ref, right_ref):
        copies = [
            pltpu.make_async_copy(left_ref, weights_ref.at[:, :fetched], sems.at[0]),
            pltpu.make_async_copy(right_ref.at[:, shared:], weights_ref.at[:, fetched:], sems.at[1]),
        ]
        for copy in copies:
            copy.start()
        for copy in copies:
            copy.wait()

    @pl.when(core_ref[0] == 0)
    def _():
        place(mine_ref, other_ref)

    @pl.when(core_ref[0] != 0)
    def _():
        place(other_ref, mine_ref)


def placed_weights(core, mine, other, columns):
    rows = mine.shape[0]
    return pl.pallas_call(
        place_kernel,
        out_shape=pltpu.VMEM((rows, columns), mine.dtype),
        in_specs=[
            pl.BlockSpec(memory_space=pltpu.SMEM),
            pl.BlockSpec(memory_space=pl.ANY),
            pl.BlockSpec(memory_space=pl.ANY),
        ],
        out_specs=pl.BlockSpec(memory_space=pltpu.VMEM),
        scratch_shapes=[pltpu.SemaphoreType.DMA((2,))],
        compiler_params=pltpu.CompilerParams(vmem_limit_bytes=16 << 20),
        cost_estimate=pl.CostEstimate(flops=0, bytes_accessed=2 * rows * columns * 2, transcendentals=0),
    )(core, *(pltpu.with_memory_space_constraint(part, pltpu.HBM) for part in (mine, other)))


def block_kernel(
    wide_columns, flags_ref, weights_ref, gain_ref, incoming_ref, fresh_ref, result_ref, own_ref, taps_ref, acts_ref
):
    rows, channels = incoming_ref.shape
    kept_rows = own_ref.shape[0]
    padded_rows = taps_ref.shape[0]
    fresh, low_half = (flags_ref[i] != 0 for i in range(2))
    acts = jnp.where(fresh, fresh_ref[...].astype(jnp.float32), incoming_ref[...].astype(jnp.float32))
    acts_ref[...] = acts
    normed = rms_scaled(acts, gain_ref[...])
    normed = jnp.concatenate([normed, jnp.zeros((padded_rows - rows, channels), jnp.float32)], axis=0)
    taps_ref[:, :channels] = pltpu.roll(normed, 1, 0).astype(jnp.bfloat16)
    taps_ref[:, channels : 2 * channels] = normed.astype(jnp.bfloat16)
    taps_ref[:, 2 * channels :] = pltpu.roll(normed, padded_rows - 1, 0).astype(jnp.bfloat16)

    def columns(at):
        mixed = jnp.dot(taps_ref[...], weights_ref[:, at], preferred_element_type=jnp.float32)
        result = acts_ref[:, at] + jax.nn.gelu(mixed[:rows])
        own = jnp.where(low_half, result[:kept_rows], result[rows - kept_rows :])
        own_ref[:, at] = own.astype(jnp.bfloat16)
        result_ref[:, at] = result.astype(jnp.bfloat16)

    whole = channels // wide_columns

    def step(i, _):
        columns(pl.ds(pl.multiple_of(i * wide_columns, wide_columns), wide_columns))
        return 0

    lax.fori_loop(0, whole, step, 0)
    if channels > whole * wide_columns:
        columns(pl.ds(whole * wide_columns, channels - whole * wide_columns))


def block(flags, weights, gains, incoming, fresh, kept_rows):
    rows, channels = incoming.shape
    padded_rows = -(-rows // 16) * 16
    vmem = pl.BlockSpec(memory_space=pltpu.VMEM)
    return pl.pallas_call(
        functools.partial(block_kernel, 256),
        out_shape=(
            jax.ShapeDtypeStruct((rows, channels), jnp.bfloat16),
            jax.ShapeDtypeStruct((kept_rows, channels), jnp.bfloat16),
        ),
        in_specs=[pl.BlockSpec(memory_space=pltpu.SMEM)] + [vmem] * 4,
        out_specs=(vmem, vmem),
        scratch_shapes=[
            pltpu.VMEM((padded_rows, weights.shape[0]), jnp.bfloat16),
            pltpu.VMEM((rows, channels), jnp.float32),
        ],
        compiler_params=pltpu.CompilerParams(vmem_limit_bytes=20 << 20),
        cost_estimate=pl.CostEstimate(
            flops=2 * rows * weights.shape[0] * channels,
            bytes_accessed=4 * rows * channels * 2,
            transcendentals=rows * channels,
        ),
    )(flags, pltpu.with_memory_space_constraint(weights, pltpu.VMEM), gains, incoming, fresh)


def on_device(
    encoded,
    conv_weight,
    section_gain,
    head_gain,
    head_weight,
    pair_donor,
    pair_acceptor,
    pair_count,
    pair_cotangent,
):
    micro_count, slab_rows, channels = encoded.shape
    sections = lax.axis_size("section")
    last = sections - 1
    section_pos = lax.axis_index("section")
    slabs = lax.axis_size("seq")
    dilation = slab_rows // 2
    half = slabs // 2
    spare = sections
    low_half = lax.axis_index("seq") < half
    halves = [list(range(half)), list(range(half, slabs))]

    fetched = -(-channels // 256) * 128
    weight_part = gathered_columns(conv_weight[0], fetched)
    def to_chains(rows):
        blocks = rows.reshape(2, dilation, channels)
        chains = lax.all_to_all(blocks, "seq", 1, 0, axis_index_groups=halves)
        return chains.reshape(slab_rows, channels)

    def to_slabs(chains):
        lead = chains.shape[:-2]
        blocks = chains.reshape(*lead, half, 2, channels)
        at = len(lead)
        rows = lax.all_to_all(blocks, "seq", at, at + 1, axis_index_groups=halves)
        return rows.reshape(*lead, slab_rows, channels)

    def own_rows(wide):
        return jnp.where(low_half, wide[..., :slab_rows, :], wide[..., spare:, :])

    mine = lax.dynamic_index_in_dim(encoded, section_pos, 0, keepdims=False)
    chains = to_chains(mine)
    edge = lax.ppermute(
        jnp.where(low_half, chains[slab_rows - spare :], chains[:spare]),
        "seq",
        [(i, (i + half) % slabs) for i in range(slabs)],
    )
    wide = jnp.where(
        low_half,
        jnp.concatenate([chains, edge], axis=0),
        jnp.concatenate([edge, chains], axis=0),
    )
    fresh = [wide if m == 0 else lax.ppermute(wide, "section", [(m, 0)]) for m in range(micro_count)]
    weight_part, *fresh = lax.optimization_barrier((weight_part, *fresh))
    core = (lax.axis_index("seq") % 2).astype(jnp.int32)
    weights = placed_weights(core[None], weight_part, core_swap(weight_part), channels)
    head_weight, weight_part = lax.optimization_barrier((head_weight, weight_part))
    head_parts = lax.all_gather(head_weight, "seq")

    def gathered_outputs(owns, first, count):
        held = jnp.stack([jnp.stack(pair) for pair in owns[first : first + count + last]])
        taken = lax.dynamic_slice_in_dim(held, section_pos, count, 0)
        return taken.reshape(2 * count, slab_rows, channels)

    pairs = micro_count // 2
    ticks = pairs + last
    early = pairs // 2
    flags = jnp.stack([section_pos == 0, low_half]).astype(jnp.int32)
    results, owns, landing, landed = [], [], [], []
    incoming = [jnp.zeros_like(wide)] * 2
    for tick in range(ticks):
        owns.append([])
        for lane in range(2):
            entered = 2 * tick + lane
            before = incoming[lane]
            if results:
                before, _ = lax.optimization_barrier((before, results[-1]))
            if len(landing) > 2:
                arrived, before = lax.optimization_barrier((landing.pop(0), before))
                landed.append(arrived)
            now = fresh[entered] if entered < micro_count else before
            result, own = block(flags, weights, section_gain, before, now, slab_rows)
            results.append(result)
            owns[-1].append(own)
            if tick < ticks - 1:
                incoming[lane] = lax.ppermute(result, "section", [(i, i + 1) for i in range(last)])
            done = entered - 2 * last
            if 0 <= done < micro_count - 1:
                leaving = jnp.where(section_pos == 0, results[done + 1], result)
                landing.append(lax.ppermute(leaving, "section", [(last, done), (0, done + 1)]))
        if tick == early - 1 + last:
            early_rows = to_slabs(gathered_outputs(owns, 0, early))
    head_input = sum(rows.astype(jnp.float32) for rows in landed + landing)
    head_input = head_input + jnp.where(section_pos == 0, results[0], 0).astype(jnp.float32)
    head_input = head_input + jnp.where(section_pos == last, results[-1], 0).astype(jnp.float32)
    embed = own_rows(rms_scaled(head_input, head_gain).astype(jnp.bfloat16))
    embed, head_parts, early_rows = lax.optimization_barrier((embed, head_parts, early_rows))
    head_full = head_parts.reshape(channels, channels)
    embed = to_slabs(embed)
    late_outputs = gathered_outputs(owns, early, pairs - early)
    embed, late_outputs = lax.optimization_barrier((embed, late_outputs))
    late_rows = to_slabs(late_outputs)
    stashed = jnp.concatenate([early_rows, late_rows], axis=0)

    scale = channels ** (-0.5)
    reach_count = pair_count.shape[2]
    capacity = pair_donor.shape[2] // reach_count
    donors = pair_donor[0, 0]
    acceptors = pair_acceptor[0, 0]
    counts = pair_count[0, 0]
    cotangents = pair_cotangent[0, 0]
    answers = jnp.take(embed, acceptors, axis=0)
    returned = [answers[:capacity]]
    for reach_idx in range(1, reach_count):
        lower = reach_idx * capacity
        returned.append(from_behind(answers[lower : lower + capacity], "seq", -reach_idx))
    queries = jnp.dot(embed, head_full, preferred_element_type=jnp.float32).astype(jnp.bfloat16)
    slot = jnp.arange(reach_count * capacity, dtype=jnp.int32)
    valid = slot % capacity < jnp.repeat(counts, capacity)
    weighted = jnp.where(valid, cotangents, jnp.zeros_like(cotangents))[:, None]
    sent = (weighted * jnp.take(queries, donors, axis=0).astype(jnp.float32) * scale).astype(
        jnp.bfloat16
    )
    received = [sent[:capacity]]
    for reach_idx in range(1, reach_count):
        lower = reach_idx * capacity
        received.append(from_behind(sent[lower : lower + capacity], "seq", reach_idx))
    received = jnp.concatenate(received, axis=0)
    returned = jnp.concatenate(returned, axis=0)
    position_index = jnp.arange(slab_rows, dtype=jnp.int32)
    accept_hot = (position_index[:, None] == acceptors[None, :]).astype(jnp.bfloat16)
    from_acc = jnp.dot(accept_hot, received, preferred_element_type=jnp.float32)
    donor_onehot = (position_index[:, None] == donors[None, :]).astype(jnp.float32)
    query_grad = jnp.dot(
        donor_onehot,
        weighted * returned.astype(jnp.float32) * scale,
        precision=lax.Precision.HIGHEST,
    )
    grad_rows = (
        lax.dot_general(
            query_grad.astype(jnp.bfloat16),
            head_full,
            (((1,), (1,)), ((), ())),
            preferred_element_type=jnp.float32,
        )
        + from_acc
    )
    return (stashed[None], grad_rows[None])


def solution(mesh):
    placed = (
        P(None, "seq", None),
        P("section", "seq", None),
        P("section", None),
        P(),
        P("seq", None),
        P("section", "seq", None),
        P("section", "seq", None),
        P("section", "seq", None),
        P("section", "seq", None),
    )
    return jax.shard_map(
        on_device,
        mesh=mesh,
        in_specs=placed,
        out_specs=(P("section", None, "seq", None), P("section", "seq", None)),
        check_vma=False,
    )
```

```python
import functools

import jax
import jax.numpy as jnp
from jax import lax
from jax.experimental import pallas as pl
from jax.experimental.pallas import tpu as pltpu
from jax.sharding import PartitionSpec as P


def from_behind(shard, axis, by):
    size = lax.axis_size(axis)
    pairs = [(i, i + by) for i in range(size) if 0 <= i + by < size]
    return lax.ppermute(shard, axis, pairs)


def rms_scaled(values, gains):
    return values * lax.rsqrt(jnp.mean(values * values, axis=-1, keepdims=True) + 1e-06) * gains


def core_swap(shard):
    return lax.ppermute(shard, "seq", [(i, i ^ 1) for i in range(lax.axis_size("seq"))])


def in_core_order(first_core, mine, other, axis):
    return jnp.where(
        first_core,
        jnp.concatenate([mine, other], axis=axis),
        jnp.concatenate([other, mine], axis=axis),
    )


def gathered_columns(shard, fetched):
    count = lax.axis_size("seq")
    columns = shard.shape[1]
    first_core = lax.axis_index("seq") % 2 == 0
    left, right = shard[:, :fetched], shard[:, columns - fetched :]
    arrived = core_swap(jnp.where(first_core, right, left))
    rows = in_core_order(first_core, jnp.where(first_core, left, right), arrived, 0)
    same_core = [list(range(core, count, 2)) for core in range(2)]
    return lax.all_gather(rows, "seq", axis_index_groups=same_core, axis=0, tiled=True)


def place_kernel(core_ref, mine_ref, other_ref, weights_ref, sems):
    fetched = mine_ref.shape[1]
    shared = 2 * fetched - weights_ref.shape[1]

    def place(left_ref, right_ref):
        copies = [
            pltpu.make_async_copy(left_ref, weights_ref.at[:, :fetched], sems.at[0]),
            pltpu.make_async_copy(right_ref.at[:, shared:], weights_ref.at[:, fetched:], sems.at[1]),
        ]
        for copy in copies:
            copy.start()
        for copy in copies:
            copy.wait()

    @pl.when(core_ref[0] == 0)
    def _():
        place(mine_ref, other_ref)

    @pl.when(core_ref[0] != 0)
    def _():
        place(other_ref, mine_ref)


def placed_weights(core, mine, other, columns):
    rows = mine.shape[0]
    return pl.pallas_call(
        place_kernel,
        out_shape=pltpu.VMEM((rows, columns), mine.dtype),
        in_specs=[
            pl.BlockSpec(memory_space=pltpu.SMEM),
            pl.BlockSpec(memory_space=pl.ANY),
            pl.BlockSpec(memory_space=pl.ANY),
        ],
        out_specs=pl.BlockSpec(memory_space=pltpu.VMEM),
        scratch_shapes=[pltpu.SemaphoreType.DMA((2,))],
        compiler_params=pltpu.CompilerParams(vmem_limit_bytes=4 << 20),
        cost_estimate=pl.CostEstimate(flops=0, bytes_accessed=2 * rows * columns * 2, transcendentals=0),
    )(core, *(pltpu.with_memory_space_constraint(part, pltpu.HBM) for part in (mine, other)))


def block_kernel(
    wide_columns, flags_ref, weights_ref, gain_ref, incoming_ref, fresh_ref, result_ref, own_ref, taps_ref, acts_ref
):
    rows, channels = incoming_ref.shape
    kept_rows = own_ref.shape[0]
    padded_rows = taps_ref.shape[0]
    fresh, low_half, active = (flags_ref[i] != 0 for i in range(3))

    def columns(at):
        mixed = jnp.dot(taps_ref[...], weights_ref[:, at], preferred_element_type=jnp.float32)
        result = acts_ref[:, at] + jax.nn.gelu(mixed[:rows])
        own = jnp.where(low_half, result[:kept_rows], result[rows - kept_rows :])
        own_ref[:, at] = own.astype(jnp.bfloat16)
        result_ref[:, at] = result.astype(jnp.bfloat16)

    @pl.when(active)
    def _():
        acts = jnp.where(
            fresh, fresh_ref[...].astype(jnp.float32), incoming_ref[...].astype(jnp.float32)
        )
        acts_ref[...] = acts
        normed = rms_scaled(acts, gain_ref[...])
        spare = jnp.zeros((padded_rows - rows, channels), jnp.float32)
        normed = jnp.concatenate([normed, spare], axis=0)
        taps_ref[:, :channels] = pltpu.roll(normed, 1, 0).astype(jnp.bfloat16)
        taps_ref[:, channels : 2 * channels] = normed.astype(jnp.bfloat16)
        taps_ref[:, 2 * channels :] = pltpu.roll(normed, padded_rows - 1, 0).astype(jnp.bfloat16)
        whole = channels // wide_columns

        def step(i, _):
            columns(pl.ds(pl.multiple_of(i * wide_columns, wide_columns), wide_columns))
            return 0

        lax.fori_loop(0, whole, step, 0)
        if channels > whole * wide_columns:
            columns(pl.ds(whole * wide_columns, channels - whole * wide_columns))

    @pl.when(jnp.logical_not(active))
    def _():
        result_ref[...] = jnp.zeros_like(result_ref)
        own_ref[...] = jnp.zeros_like(own_ref)


def block(flags, weights, gains, incoming, fresh, kept_rows):
    rows, channels = incoming.shape
    padded_rows = -(-rows // 16) * 16
    vmem = pl.BlockSpec(memory_space=pltpu.VMEM)
    return pl.pallas_call(
        functools.partial(block_kernel, 256),
        out_shape=(
            jax.ShapeDtypeStruct((rows, channels), jnp.bfloat16),
            jax.ShapeDtypeStruct((kept_rows, channels), jnp.bfloat16),
        ),
        in_specs=[pl.BlockSpec(memory_space=pltpu.SMEM)] + [vmem] * 4,
        out_specs=(vmem, vmem),
        scratch_shapes=[
            pltpu.VMEM((padded_rows, weights.shape[0]), jnp.bfloat16),
            pltpu.VMEM((rows, channels), jnp.float32),
        ],
        compiler_params=pltpu.CompilerParams(vmem_limit_bytes=8 << 20),
        cost_estimate=pl.CostEstimate(
            flops=2 * rows * weights.shape[0] * channels,
            bytes_accessed=4 * rows * channels * 2,
            transcendentals=rows * channels,
        ),
    )(flags, pltpu.with_memory_space_constraint(weights, pltpu.VMEM), gains, incoming, fresh)


def on_device(
    encoded,
    conv_weight,
    section_gain,
    head_gain,
    head_weight,
    pair_donor,
    pair_acceptor,
    pair_count,
    pair_cotangent,
):
    micro_count, slab_rows, channels = encoded.shape
    sections = lax.axis_size("section")
    last = sections - 1
    section_pos = lax.axis_index("section")
    slabs = lax.axis_size("seq")
    dilation = slab_rows // 2
    half = slabs // 2
    spare = sections
    low_half = lax.axis_index("seq") < half
    halves = [list(range(half)), list(range(half, slabs))]

    fetched = -(-channels // 256) * 128
    weight_part = gathered_columns(conv_weight[0], fetched)
    def to_chains(rows):
        blocks = rows.reshape(2, dilation, channels)
        chains = lax.all_to_all(blocks, "seq", 1, 0, axis_index_groups=halves)
        return chains.reshape(slab_rows, channels)

    def to_slabs(chains):
        lead = chains.shape[:-2]
        blocks = chains.reshape(*lead, half, 2, channels)
        at = len(lead)
        rows = lax.all_to_all(blocks, "seq", at, at + 1, axis_index_groups=halves)
        return rows.reshape(*lead, slab_rows, channels)

    def own_rows(wide):
        return jnp.where(low_half, wide[..., :slab_rows, :], wide[..., spare:, :])

    mine = lax.dynamic_index_in_dim(encoded, section_pos, 0, keepdims=False)
    chains = to_chains(mine)
    edge = lax.ppermute(
        jnp.where(low_half, chains[slab_rows - spare :], chains[:spare]),
        "seq",
        [(i, (i + half) % slabs) for i in range(slabs)],
    )
    wide = jnp.where(
        low_half,
        jnp.concatenate([chains, edge], axis=0),
        jnp.concatenate([edge, chains], axis=0),
    )
    fresh = [wide if m == 0 else lax.ppermute(wide, "section", [(m, 0)]) for m in range(micro_count)]
    weight_part, *fresh = lax.optimization_barrier((weight_part, *fresh))
    core = (lax.axis_index("seq") % 2).astype(jnp.int32)
    weights = placed_weights(core[None], weight_part, core_swap(weight_part), channels)
    head_weight, weight_part = lax.optimization_barrier((head_weight, weight_part))
    head_parts = lax.all_gather(head_weight, "seq")

    def gathered_outputs(owns, first, count):
        held = jnp.stack([jnp.stack(pair) for pair in owns[first : first + count + last]])
        taken = lax.dynamic_slice_in_dim(held, section_pos, count, 0)
        return taken.reshape(2 * count, slab_rows, channels)

    pairs = micro_count // 2
    ticks = pairs + last
    early = pairs // 2
    results, owns, landing, landed = [], [], [], []
    incoming = [jnp.zeros_like(wide)] * 2
    for tick in range(ticks):
        owns.append([])
        busy = [i for i in range(sections) if 0 <= tick - i < pairs]
        active = (section_pos >= busy[0]) & (section_pos <= busy[-1])
        flags = jnp.stack([section_pos == 0, low_half, active]).astype(jnp.int32)
        for lane in range(2):
            entered = 2 * tick + lane
            before = incoming[lane]
            if results:
                before, _ = lax.optimization_barrier((before, results[-1]))
            if len(landing) > 2:
                arrived, before = lax.optimization_barrier((landing.pop(0), before))
                landed.append(arrived)
            now = fresh[entered] if entered < micro_count else before
            result, own = block(flags, weights, section_gain, before, now, slab_rows)
            results.append(result)
            owns[-1].append(own)
            if tick < ticks - 1:
                incoming[lane] = lax.ppermute(
                    result, "section", [(i, i + 1) for i in busy if i < last]
                )
            done = entered - 2 * last
            if 0 <= done < micro_count - 1:
                leaving = jnp.where(section_pos == 0, results[done + 1], result)
                landing.append(lax.ppermute(leaving, "section", [(last, done), (0, done + 1)]))
        if tick == early - 1 + last:
            early_rows = to_slabs(gathered_outputs(owns, 0, early))
    head_input = sum(rows.astype(jnp.float32) for rows in landed + landing)
    head_input = head_input + jnp.where(section_pos == 0, results[0], 0).astype(jnp.float32)
    head_input = head_input + jnp.where(section_pos == last, results[-1], 0).astype(jnp.float32)
    embed = own_rows(rms_scaled(head_input, head_gain).astype(jnp.bfloat16))
    embed, head_parts, early_rows = lax.optimization_barrier((embed, head_parts, early_rows))
    head_full = head_parts.reshape(channels, channels)
    embed = to_slabs(embed)
    late_outputs = gathered_outputs(owns, early, pairs - early)
    embed, late_outputs = lax.optimization_barrier((embed, late_outputs))
    late_rows = to_slabs(late_outputs)
    stashed = jnp.concatenate([early_rows, late_rows], axis=0)

    scale = channels ** (-0.5)
    reach_count = pair_count.shape[2]
    capacity = pair_donor.shape[2] // reach_count
    donors = pair_donor[0, 0]
    acceptors = pair_acceptor[0, 0]
    counts = pair_count[0, 0]
    cotangents = pair_cotangent[0, 0]
    answers = jnp.take(embed, acceptors, axis=0)
    returned = [answers[:capacity]]
    for reach_idx in range(1, reach_count):
        lower = reach_idx * capacity
        returned.append(from_behind(answers[lower : lower + capacity], "seq", -reach_idx))
    queries = jnp.dot(embed, head_full, preferred_element_type=jnp.float32).astype(jnp.bfloat16)
    slot = jnp.arange(reach_count * capacity, dtype=jnp.int32)
    valid = slot % capacity < jnp.repeat(counts, capacity)
    weighted = jnp.where(valid, cotangents, jnp.zeros_like(cotangents))[:, None]
    sent = (weighted * jnp.take(queries, donors, axis=0).astype(jnp.float32) * scale).astype(
        jnp.bfloat16
    )
    received = [sent[:capacity]]
    for reach_idx in range(1, reach_count):
        lower = reach_idx * capacity
        received.append(from_behind(sent[lower : lower + capacity], "seq", reach_idx))
    received = jnp.concatenate(received, axis=0)
    returned = jnp.concatenate(returned, axis=0)
    position_index = jnp.arange(slab_rows, dtype=jnp.int32)
    accept_hot = (position_index[:, None] == acceptors[None, :]).astype(jnp.bfloat16)
    from_acc = jnp.dot(accept_hot, received, preferred_element_type=jnp.float32)
    donor_onehot = (position_index[:, None] == donors[None, :]).astype(jnp.float32)
    query_grad = jnp.dot(
        donor_onehot,
        weighted * returned.astype(jnp.float32) * scale,
        precision=lax.Precision.HIGHEST,
    )
    grad_rows = (
        lax.dot_general(
            query_grad.astype(jnp.bfloat16),
            head_full,
            (((1,), (1,)), ((), ())),
            preferred_element_type=jnp.float32,
        )
        + from_acc
    )
    return (stashed[None], grad_rows[None])


def solution(mesh):
    placed = (
        P(None, "seq", None),
        P("section", "seq", None),
        P("section", None),
        P(),
        P("seq", None),
        P("section", "seq", None),
        P("section", "seq", None),
        P("section", "seq", None),
        P("section", "seq", None),
    )
    return jax.shard_map(
        on_device,
        mesh=mesh,
        in_specs=placed,
        out_specs=(P("section", None, "seq", None), P("section", "seq", None)),
        check_vma=False,
    )
```

```python
import functools

import jax
import jax.numpy as jnp
from jax import lax
from jax.experimental import pallas as pl
from jax.experimental.pallas import tpu as pltpu
from jax.sharding import PartitionSpec as P


def from_behind(shard, axis, by):
    size = lax.axis_size(axis)
    pairs = [(i, i + by) for i in range(size) if 0 <= i + by < size]
    return lax.ppermute(shard, axis, pairs)


def rms_scaled(values, gains):
    return values * lax.rsqrt(jnp.mean(values * values, axis=-1, keepdims=True) + 1e-06) * gains


def core_swap(shard):
    return lax.ppermute(shard, "seq", [(i, i ^ 1) for i in range(lax.axis_size("seq"))])


def in_core_order(first_core, mine, other, axis):
    return jnp.where(
        first_core,
        jnp.concatenate([mine, other], axis=axis),
        jnp.concatenate([other, mine], axis=axis),
    )


def gathered_columns(shard, fetched):
    count = lax.axis_size("seq")
    columns = shard.shape[1]
    first_core = lax.axis_index("seq") % 2 == 0
    left, right = shard[:, :fetched], shard[:, columns - fetched :]
    arrived = core_swap(jnp.where(first_core, right, left))
    rows = in_core_order(first_core, jnp.where(first_core, left, right), arrived, 0)
    same_core = [list(range(core, count, 2)) for core in range(2)]
    return lax.all_gather(rows, "seq", axis_index_groups=same_core, axis=0, tiled=True)


def place_kernel(core_ref, mine_ref, other_ref, weights_ref, sems):
    fetched = mine_ref.shape[1]
    shared = 2 * fetched - weights_ref.shape[1]

    def place(left_ref, right_ref):
        copies = [
            pltpu.make_async_copy(left_ref, weights_ref.at[:, :fetched], sems.at[0]),
            pltpu.make_async_copy(right_ref.at[:, shared:], weights_ref.at[:, fetched:], sems.at[1]),
        ]
        for copy in copies:
            copy.start()
        for copy in copies:
            copy.wait()

    @pl.when(core_ref[0] == 0)
    def _():
        place(mine_ref, other_ref)

    @pl.when(core_ref[0] != 0)
    def _():
        place(other_ref, mine_ref)


def placed_weights(core, mine, other, columns):
    rows = mine.shape[0]
    return pl.pallas_call(
        place_kernel,
        out_shape=pltpu.VMEM((rows, columns), mine.dtype),
        in_specs=[
            pl.BlockSpec(memory_space=pltpu.SMEM),
            pl.BlockSpec(memory_space=pl.ANY),
            pl.BlockSpec(memory_space=pl.ANY),
        ],
        out_specs=pl.BlockSpec(memory_space=pltpu.VMEM),
        scratch_shapes=[pltpu.SemaphoreType.DMA((2,))],
        compiler_params=pltpu.CompilerParams(vmem_limit_bytes=4 << 20),
        cost_estimate=pl.CostEstimate(flops=0, bytes_accessed=2 * rows * columns * 2, transcendentals=0),
    )(core, *(pltpu.with_memory_space_constraint(part, pltpu.HBM) for part in (mine, other)))


def block_kernel(
    wide_columns, flags_ref, weights_ref, gain_ref, incoming_ref, fresh_ref, result_ref, own_ref, taps_ref, acts_ref
):
    rows, channels = incoming_ref.shape
    kept_rows = own_ref.shape[0]
    padded_rows = taps_ref.shape[0]
    fresh, low_half, active = (flags_ref[i] != 0 for i in range(3))

    def columns(at):
        mixed = jnp.dot(taps_ref[...], weights_ref[:, at], preferred_element_type=jnp.float32)
        result = acts_ref[:, at] + jax.nn.gelu(mixed[:rows])
        own = jnp.where(low_half, result[:kept_rows], result[rows - kept_rows :])
        own_ref[:, at] = own.astype(jnp.bfloat16)
        result_ref[:, at] = result.astype(jnp.bfloat16)

    @pl.when(active)
    def _():
        acts = jnp.where(
            fresh, fresh_ref[...].astype(jnp.float32), incoming_ref[...].astype(jnp.float32)
        )
        acts_ref[...] = acts
        normed = rms_scaled(acts, gain_ref[...])
        spare = jnp.zeros((padded_rows - rows, channels), jnp.float32)
        normed = jnp.concatenate([normed, spare], axis=0)
        taps_ref[:, :channels] = pltpu.roll(normed, 1, 0).astype(jnp.bfloat16)
        taps_ref[:, channels : 2 * channels] = normed.astype(jnp.bfloat16)
        taps_ref[:, 2 * channels :] = pltpu.roll(normed, padded_rows - 1, 0).astype(jnp.bfloat16)
        whole = channels // wide_columns

        def step(i, _):
            columns(pl.ds(pl.multiple_of(i * wide_columns, wide_columns), wide_columns))
            return 0

        lax.fori_loop(0, whole, step, 0)
        if channels > whole * wide_columns:
            columns(pl.ds(whole * wide_columns, channels - whole * wide_columns))

    @pl.when(jnp.logical_not(active))
    def _():
        result_ref[...] = jnp.zeros_like(result_ref)
        own_ref[...] = jnp.zeros_like(own_ref)


def block(flags, weights, gains, incoming, fresh, kept_rows):
    rows, channels = incoming.shape
    padded_rows = -(-rows // 16) * 16
    vmem = pl.BlockSpec(memory_space=pltpu.VMEM)
    return pl.pallas_call(
        functools.partial(block_kernel, 256),
        out_shape=(
            jax.ShapeDtypeStruct((rows, channels), jnp.bfloat16),
            jax.ShapeDtypeStruct((kept_rows, channels), jnp.bfloat16),
        ),
        in_specs=[pl.BlockSpec(memory_space=pltpu.SMEM)] + [vmem] * 4,
        out_specs=(vmem, vmem),
        scratch_shapes=[
            pltpu.VMEM((padded_rows, weights.shape[0]), jnp.bfloat16),
            pltpu.VMEM((rows, channels), jnp.float32),
        ],
        compiler_params=pltpu.CompilerParams(vmem_limit_bytes=8 << 20),
        cost_estimate=pl.CostEstimate(
            flops=2 * rows * weights.shape[0] * channels,
            bytes_accessed=4 * rows * channels * 2,
            transcendentals=rows * channels,
        ),
    )(flags, pltpu.with_memory_space_constraint(weights, pltpu.VMEM), gains, incoming, fresh)


def on_device(
    encoded,
    conv_weight,
    section_gain,
    head_gain,
    head_weight,
    pair_donor,
    pair_acceptor,
    pair_count,
    pair_cotangent,
):
    micro_count, slab_rows, channels = encoded.shape
    sections = lax.axis_size("section")
    last = sections - 1
    section_pos = lax.axis_index("section")
    slabs = lax.axis_size("seq")
    dilation = slab_rows // 2
    half = slabs // 2
    spare = sections
    low_half = lax.axis_index("seq") < half
    halves = [list(range(half)), list(range(half, slabs))]

    fetched = -(-channels // 256) * 128
    weight_part = gathered_columns(conv_weight[0], fetched)
    def to_chains(rows):
        blocks = rows.reshape(2, dilation, channels)
        chains = lax.all_to_all(blocks, "seq", 1, 0, axis_index_groups=halves)
        return chains.reshape(slab_rows, channels)

    def to_slabs(chains):
        lead = chains.shape[:-2]
        blocks = chains.reshape(*lead, half, 2, channels)
        at = len(lead)
        rows = lax.all_to_all(blocks, "seq", at, at + 1, axis_index_groups=halves)
        return rows.reshape(*lead, slab_rows, channels)

    def own_rows(wide):
        return jnp.where(low_half, wide[..., :slab_rows, :], wide[..., spare:, :])

    mine = lax.dynamic_index_in_dim(encoded, section_pos, 0, keepdims=False)
    chains = to_chains(mine)
    edge = lax.ppermute(
        jnp.where(low_half, chains[slab_rows - spare :], chains[:spare]),
        "seq",
        [(i, (i + half) % slabs) for i in range(slabs)],
    )
    wide = jnp.where(
        low_half,
        jnp.concatenate([chains, edge], axis=0),
        jnp.concatenate([edge, chains], axis=0),
    )
    held, reach = wide[None], 1
    while reach < micro_count:
        sent = [(m, m - reach) for m in range(reach, micro_count, 2 * reach)]
        held = jnp.concatenate([held, lax.ppermute(held, "section", sent)], axis=0)
        reach *= 2
    fresh = [held[m] for m in range(micro_count)]
    weight_part, *fresh = lax.optimization_barrier((weight_part, *fresh))
    core = (lax.axis_index("seq") % 2).astype(jnp.int32)
    weights = placed_weights(core[None], weight_part, core_swap(weight_part), channels)
    head_weight, weight_part = lax.optimization_barrier((head_weight, weight_part))
    head_parts = lax.all_gather(head_weight, "seq")

    def gathered_outputs(owns, first, count):
        held = jnp.stack([jnp.stack(pair) for pair in owns[first : first + count + last]])
        taken = lax.dynamic_slice_in_dim(held, section_pos, count, 0)
        return taken.reshape(2 * count, slab_rows, channels)

    pairs = micro_count // 2
    ticks = pairs + last
    early = pairs // 2
    results, owns, landing, landed = [], [], [], []
    incoming = [jnp.zeros_like(wide)] * 2
    for tick in range(ticks):
        owns.append([])
        busy = [i for i in range(sections) if 0 <= tick - i < pairs]
        senders = last - pairs if tick >= last - 1 else 0
        active = (section_pos >= busy[0]) & (section_pos <= busy[-1])
        flags = jnp.stack([section_pos == 0, low_half, active]).astype(jnp.int32)
        for lane in range(2):
            entered = 2 * tick + lane
            before = incoming[lane]
            if results:
                before, _ = lax.optimization_barrier((before, results[-1]))
            if len(landing) > 2:
                arrived, before = lax.optimization_barrier((landing.pop(0), before))
                landed.append(arrived)
            now = fresh[entered] if entered < micro_count else before
            result, own = block(flags, weights, section_gain, before, now, slab_rows)
            results.append(result)
            owns[-1].append(own)
            if tick < ticks - 1:
                incoming[lane] = lax.ppermute(
                    result, "section", [(i, i + 1) for i in range(senders, last)]
                )
            done = entered - 2 * last
            if 0 <= done < micro_count - 1:
                leaving = jnp.where(section_pos == 0, results[done + 1], result)
                landing.append(lax.ppermute(leaving, "section", [(last, done), (0, done + 1)]))
        if tick == early - 1 + last:
            early_rows = to_slabs(gathered_outputs(owns, 0, early))
    head_input = sum(rows.astype(jnp.float32) for rows in landed + landing)
    head_input = head_input + jnp.where(section_pos == 0, results[0], 0).astype(jnp.float32)
    head_input = head_input + jnp.where(section_pos == last, results[-1], 0).astype(jnp.float32)
    embed = own_rows(rms_scaled(head_input, head_gain).astype(jnp.bfloat16))
    embed, head_parts, early_rows = lax.optimization_barrier((embed, head_parts, early_rows))
    head_full = head_parts.reshape(channels, channels)
    embed = to_slabs(embed)
    late_outputs = gathered_outputs(owns, early, pairs - early)
    embed, late_outputs = lax.optimization_barrier((embed, late_outputs))
    late_rows = to_slabs(late_outputs)
    stashed = jnp.concatenate([early_rows, late_rows], axis=0)

    scale = channels ** (-0.5)
    reach_count = pair_count.shape[2]
    capacity = pair_donor.shape[2] // reach_count
    donors = pair_donor[0, 0]
    acceptors = pair_acceptor[0, 0]
    counts = pair_count[0, 0]
    cotangents = pair_cotangent[0, 0]
    answers = jnp.take(embed, acceptors, axis=0)
    returned = [answers[:capacity]]
    for reach_idx in range(1, reach_count):
        lower = reach_idx * capacity
        returned.append(from_behind(answers[lower : lower + capacity], "seq", -reach_idx))
    queries = jnp.dot(embed, head_full, preferred_element_type=jnp.float32).astype(jnp.bfloat16)
    slot = jnp.arange(reach_count * capacity, dtype=jnp.int32)
    valid = slot % capacity < jnp.repeat(counts, capacity)
    weighted = jnp.where(valid, cotangents, jnp.zeros_like(cotangents))[:, None]
    sent = (weighted * jnp.take(queries, donors, axis=0).astype(jnp.float32) * scale).astype(
        jnp.bfloat16
    )
    received = [sent[:capacity]]
    for reach_idx in range(1, reach_count):
        lower = reach_idx * capacity
        received.append(from_behind(sent[lower : lower + capacity], "seq", reach_idx))
    received = jnp.concatenate(received, axis=0)
    returned = jnp.concatenate(returned, axis=0)
    position_index = jnp.arange(slab_rows, dtype=jnp.int32)
    accept_hot = (position_index[:, None] == acceptors[None, :]).astype(jnp.bfloat16)
    from_acc = jnp.dot(accept_hot, received, preferred_element_type=jnp.float32)
    donor_onehot = (position_index[:, None] == donors[None, :]).astype(jnp.float32)
    query_grad = jnp.dot(
        donor_onehot,
        weighted * returned.astype(jnp.float32) * scale,
        precision=lax.Precision.HIGHEST,
    )
    grad_rows = (
        lax.dot_general(
            query_grad.astype(jnp.bfloat16),
            head_full,
            (((1,), (1,)), ((), ())),
            preferred_element_type=jnp.float32,
        )
        + from_acc
    )
    return (stashed[None], grad_rows[None])


def solution(mesh):
    placed = (
        P(None, "seq", None),
        P("section", "seq", None),
        P("section", None),
        P(),
        P("seq", None),
        P("section", "seq", None),
        P("section", "seq", None),
        P("section", "seq", None),
        P("section", "seq", None),
    )
    return jax.shard_map(
        on_device,
        mesh=mesh,
        in_specs=placed,
        out_specs=(P("section", None, "seq", None), P("section", "seq", None)),
        check_vma=False,
    )
```

```python
import functools

import jax
import jax.numpy as jnp
from jax import lax
from jax.experimental import pallas as pl
from jax.experimental.pallas import tpu as pltpu
from jax.sharding import PartitionSpec as P


def from_behind(shard, axis, by):
    size = lax.axis_size(axis)
    pairs = [(i, i + by) for i in range(size) if 0 <= i + by < size]
    return lax.ppermute(shard, axis, pairs)


def rms_scaled(values, gains):
    return values * lax.rsqrt(jnp.mean(values * values, axis=-1, keepdims=True) + 1e-06) * gains


def core_swap(shard):
    return lax.ppermute(shard, "seq", [(i, i ^ 1) for i in range(lax.axis_size("seq"))])


def in_core_order(first_core, mine, other, axis):
    return jnp.where(
        first_core,
        jnp.concatenate([mine, other], axis=axis),
        jnp.concatenate([other, mine], axis=axis),
    )


def gathered_columns(shard, fetched):
    count = lax.axis_size("seq")
    columns = shard.shape[1]
    first_core = lax.axis_index("seq") % 2 == 0
    left, right = shard[:, :fetched], shard[:, columns - fetched :]
    arrived = core_swap(jnp.where(first_core, right, left))
    rows = in_core_order(first_core, jnp.where(first_core, left, right), arrived, 0)
    same_core = [list(range(core, count, 2)) for core in range(2)]
    return lax.all_gather(rows, "seq", axis_index_groups=same_core, axis=0, tiled=True)


def place_kernel(core_ref, mine_ref, other_ref, weights_ref, sems):
    fetched = mine_ref.shape[1]
    shared = 2 * fetched - weights_ref.shape[1]

    def place(left_ref, right_ref):
        copies = [
            pltpu.make_async_copy(left_ref, weights_ref.at[:, :fetched], sems.at[0]),
            pltpu.make_async_copy(right_ref.at[:, shared:], weights_ref.at[:, fetched:], sems.at[1]),
        ]
        for copy in copies:
            copy.start()
        for copy in copies:
            copy.wait()

    @pl.when(core_ref[0] == 0)
    def _():
        place(mine_ref, other_ref)

    @pl.when(core_ref[0] != 0)
    def _():
        place(other_ref, mine_ref)


def placed_weights(core, mine, other, columns):
    rows = mine.shape[0]
    return pl.pallas_call(
        place_kernel,
        out_shape=pltpu.VMEM((rows, columns), mine.dtype),
        in_specs=[
            pl.BlockSpec(memory_space=pltpu.SMEM),
            pl.BlockSpec(memory_space=pl.ANY),
            pl.BlockSpec(memory_space=pl.ANY),
        ],
        out_specs=pl.BlockSpec(memory_space=pltpu.VMEM),
        scratch_shapes=[pltpu.SemaphoreType.DMA((2,))],
        compiler_params=pltpu.CompilerParams(vmem_limit_bytes=4 << 20),
        cost_estimate=pl.CostEstimate(flops=0, bytes_accessed=2 * rows * columns * 2, transcendentals=0),
    )(core, *(pltpu.with_memory_space_constraint(part, pltpu.HBM) for part in (mine, other)))


def block_kernel(
    wide_columns, flags_ref, weights_ref, gain_ref, incoming_ref, fresh_ref, result_ref, own_ref, taps_ref, acts_ref
):
    rows, channels = incoming_ref.shape
    kept_rows = own_ref.shape[0]
    padded_rows = taps_ref.shape[0]
    fresh, low_half, active = (flags_ref[i] != 0 for i in range(3))

    def columns(at):
        mixed = jnp.dot(taps_ref[...], weights_ref[:, at], preferred_element_type=jnp.float32)
        result = acts_ref[:, at] + jax.nn.gelu(mixed[:rows])
        own = jnp.where(low_half, result[:kept_rows], result[rows - kept_rows :])
        own_ref[:, at] = own.astype(jnp.bfloat16)
        result_ref[:, at] = result.astype(jnp.bfloat16)

    @pl.when(active)
    def _():
        acts = jnp.where(
            fresh, fresh_ref[...].astype(jnp.float32), incoming_ref[...].astype(jnp.float32)
        )
        acts_ref[...] = acts
        normed = rms_scaled(acts, gain_ref[...])
        spare = jnp.zeros((padded_rows - rows, channels), jnp.float32)
        normed = jnp.concatenate([normed, spare], axis=0)
        taps_ref[:, :channels] = pltpu.roll(normed, 1, 0).astype(jnp.bfloat16)
        taps_ref[:, channels : 2 * channels] = normed.astype(jnp.bfloat16)
        taps_ref[:, 2 * channels :] = pltpu.roll(normed, padded_rows - 1, 0).astype(jnp.bfloat16)
        whole = channels // wide_columns

        def step(i, _):
            columns(pl.ds(pl.multiple_of(i * wide_columns, wide_columns), wide_columns))
            return 0

        lax.fori_loop(0, whole, step, 0)
        if channels > whole * wide_columns:
            columns(pl.ds(whole * wide_columns, channels - whole * wide_columns))

    @pl.when(jnp.logical_not(active))
    def _():
        result_ref[...] = jnp.zeros_like(result_ref)
        own_ref[...] = jnp.zeros_like(own_ref)


def block(flags, weights, gains, incoming, fresh, kept_rows):
    rows, channels = incoming.shape
    padded_rows = -(-rows // 16) * 16
    vmem = pl.BlockSpec(memory_space=pltpu.VMEM)
    return pl.pallas_call(
        functools.partial(block_kernel, 256),
        out_shape=(
            jax.ShapeDtypeStruct((rows, channels), jnp.bfloat16),
            jax.ShapeDtypeStruct((kept_rows, channels), jnp.bfloat16),
        ),
        in_specs=[pl.BlockSpec(memory_space=pltpu.SMEM)] + [vmem] * 4,
        out_specs=(vmem, vmem),
        scratch_shapes=[
            pltpu.VMEM((padded_rows, weights.shape[0]), jnp.bfloat16),
            pltpu.VMEM((rows, channels), jnp.float32),
        ],
        compiler_params=pltpu.CompilerParams(vmem_limit_bytes=8 << 20),
        cost_estimate=pl.CostEstimate(
            flops=2 * rows * weights.shape[0] * channels,
            bytes_accessed=4 * rows * channels * 2,
            transcendentals=rows * channels,
        ),
    )(flags, pltpu.with_memory_space_constraint(weights, pltpu.VMEM), gains, incoming, fresh)


def on_device(
    encoded,
    conv_weight,
    section_gain,
    head_gain,
    head_weight,
    pair_donor,
    pair_acceptor,
    pair_count,
    pair_cotangent,
):
    micro_count, slab_rows, channels = encoded.shape
    sections = lax.axis_size("section")
    last = sections - 1
    section_pos = lax.axis_index("section")
    slabs = lax.axis_size("seq")
    dilation = slab_rows // 2
    half = slabs // 2
    spare = sections
    low_half = lax.axis_index("seq") < half
    halves = [list(range(half)), list(range(half, slabs))]

    fetched = -(-channels // 256) * 128
    weight_part = gathered_columns(conv_weight[0], fetched)
    def to_chains(rows):
        blocks = rows.reshape(2, dilation, channels)
        chains = lax.all_to_all(blocks, "seq", 1, 0, axis_index_groups=halves)
        return chains.reshape(slab_rows, channels)

    def to_slabs(chains):
        lead = chains.shape[:-2]
        blocks = chains.reshape(*lead, half, 2, channels)
        at = len(lead)
        rows = lax.all_to_all(blocks, "seq", at, at + 1, axis_index_groups=halves)
        return rows.reshape(*lead, slab_rows, channels)

    def own_rows(wide):
        return jnp.where(low_half, wide[..., :slab_rows, :], wide[..., spare:, :])

    mine = lax.dynamic_index_in_dim(encoded, section_pos, 0, keepdims=False)
    chains = to_chains(mine)
    edge = lax.ppermute(
        jnp.where(low_half, chains[slab_rows - spare :], chains[:spare]),
        "seq",
        [(i, (i + half) % slabs) for i in range(slabs)],
    )
    wide = jnp.where(
        low_half,
        jnp.concatenate([chains, edge], axis=0),
        jnp.concatenate([edge, chains], axis=0),
    )
    held, reach = wide[None], 1
    while reach < micro_count:
        sent = [(m, m - reach) for m in range(reach, micro_count, 2 * reach)]
        held = jnp.concatenate([held, lax.ppermute(held, "section", sent)], axis=0)
        reach *= 2
    fresh = [held[m] for m in range(micro_count)]
    weight_part, *fresh = lax.optimization_barrier((weight_part, *fresh))
    core = (lax.axis_index("seq") % 2).astype(jnp.int32)
    weights = placed_weights(core[None], weight_part, core_swap(weight_part), channels)
    head_weight, weight_part = lax.optimization_barrier((head_weight, weight_part))
    head_parts = lax.all_gather(head_weight, "seq")

    def gathered_outputs(owns, first, count):
        held = jnp.stack([jnp.stack(pair) for pair in owns[first : first + count + last]])
        taken = lax.dynamic_slice_in_dim(held, section_pos, count, 0)
        return taken.reshape(2 * count, slab_rows, channels)

    pairs = micro_count // 2
    ticks = pairs + last
    early = pairs // 2
    results, owns, landing, landed = [], [], [], []
    incoming = [jnp.zeros_like(wide)] * 2
    for tick in range(ticks):
        owns.append([])
        busy = [i for i in range(sections) if 0 <= tick - i < pairs]
        senders = last - pairs if tick >= last - 1 else 0
        active = (section_pos >= busy[0]) & (section_pos <= busy[-1])
        flags = jnp.stack([section_pos == 0, low_half, active]).astype(jnp.int32)
        for lane in range(2):
            entered = 2 * tick + lane
            before = incoming[lane]
            if results:
                before, _ = lax.optimization_barrier((before, results[-1]))
            if len(landing) > 4:
                arrived, before = lax.optimization_barrier((landing.pop(0), before))
                landed.append(arrived)
            now = fresh[entered] if entered < micro_count else before
            result, own = block(flags, weights, section_gain, before, now, slab_rows)
            results.append(result)
            owns[-1].append(own)
            if tick < ticks - 1:
                incoming[lane] = lax.ppermute(
                    result, "section", [(i, i + 1) for i in range(senders, last)]
                )
            done = entered - 2 * last
            if 0 <= done < micro_count - 1:
                leaving = jnp.where(section_pos == 0, results[done + 1], result)
                landing.append(lax.ppermute(leaving, "section", [(last, done), (0, done + 1)]))
        if tick == early - 1 + last:
            early_rows = to_slabs(gathered_outputs(owns, 0, early))
    head_input = sum(rows.astype(jnp.float32) for rows in landed + landing)
    head_input = head_input + jnp.where(section_pos == 0, results[0], 0).astype(jnp.float32)
    head_input = head_input + jnp.where(section_pos == last, results[-1], 0).astype(jnp.float32)
    embed = own_rows(rms_scaled(head_input, head_gain).astype(jnp.bfloat16))
    embed, head_parts, early_rows = lax.optimization_barrier((embed, head_parts, early_rows))
    head_full = head_parts.reshape(channels, channels)
    embed = to_slabs(embed)
    late_outputs = gathered_outputs(owns, early, pairs - early)
    embed, late_outputs = lax.optimization_barrier((embed, late_outputs))
    late_rows = to_slabs(late_outputs)
    stashed = jnp.concatenate([early_rows, late_rows], axis=0)

    scale = channels ** (-0.5)
    reach_count = pair_count.shape[2]
    capacity = pair_donor.shape[2] // reach_count
    donors = pair_donor[0, 0]
    acceptors = pair_acceptor[0, 0]
    counts = pair_count[0, 0]
    cotangents = pair_cotangent[0, 0]
    answers = jnp.take(embed, acceptors, axis=0)
    returned = [answers[:capacity]]
    for reach_idx in range(1, reach_count):
        lower = reach_idx * capacity
        returned.append(from_behind(answers[lower : lower + capacity], "seq", -reach_idx))
    queries = jnp.dot(embed, head_full, preferred_element_type=jnp.float32).astype(jnp.bfloat16)
    slot = jnp.arange(reach_count * capacity, dtype=jnp.int32)
    valid = slot % capacity < jnp.repeat(counts, capacity)
    weighted = jnp.where(valid, cotangents, jnp.zeros_like(cotangents))[:, None]
    sent = (weighted * jnp.take(queries, donors, axis=0).astype(jnp.float32) * scale).astype(
        jnp.bfloat16
    )
    received = [sent[:capacity]]
    for reach_idx in range(1, reach_count):
        lower = reach_idx * capacity
        received.append(from_behind(sent[lower : lower + capacity], "seq", reach_idx))
    received = jnp.concatenate(received, axis=0)
    returned = jnp.concatenate(returned, axis=0)
    position_index = jnp.arange(slab_rows, dtype=jnp.int32)
    accept_hot = (position_index[:, None] == acceptors[None, :]).astype(jnp.bfloat16)
    from_acc = jnp.dot(accept_hot, received, preferred_element_type=jnp.float32)
    donor_onehot = (position_index[:, None] == donors[None, :]).astype(jnp.float32)
    query_grad = jnp.dot(
        donor_onehot,
        weighted * returned.astype(jnp.float32) * scale,
        precision=lax.Precision.HIGHEST,
    )
    grad_rows = (
        lax.dot_general(
            query_grad.astype(jnp.bfloat16),
            head_full,
            (((1,), (1,)), ((), ())),
            preferred_element_type=jnp.float32,
        )
        + from_acc
    )
    return (stashed[None], grad_rows[None])


def solution(mesh):
    placed = (
        P(None, "seq", None),
        P("section", "seq", None),
        P("section", None),
        P(),
        P("seq", None),
        P("section", "seq", None),
        P("section", "seq", None),
        P("section", "seq", None),
        P("section", "seq", None),
    )
    return jax.shard_map(
        on_device,
        mesh=mesh,
        in_specs=placed,
        out_specs=(P("section", None, "seq", None), P("section", "seq", None)),
        check_vma=False,
    )
```
